256 devices in a mesh: dp: 8 (over x, core), space: 8 (over y, z_lo), chan: 4 (over z_hi).
Axes of the slice: x: 4, y: 4, z: 8 (z_hi: 4, z_lo: 2; z = z_hi * 2 + z_lo), core: 2. Of those that a mesh axis runs over, the one named last changes fastest.
Arguments:
- inputs: bfloat16 [8, 64, 16, 8, 128], P('dp', 'chan', 'space'), may hold values from -6 to 6
- pre_one: bfloat16 [8, 128, 16, 8, 128], P('dp', 'chan', 'space'), may hold values from -6 to 6
- pre_two: bfloat16 [8, 128, 16, 8, 128], P('dp', 'chan', 'space'), may hold values from -6 to 6
- grad_out: bfloat16 [8, 128, 16, 8, 128], P('dp', 'chan', 'space'), may hold values from -6 to 6
- weight_one: bfloat16 [128, 27, 64], P('chan'), may hold values from -0.21875 to 0.21875
- weight_two: bfloat16 [128, 27, 128], P('chan'), may hold values from -0.125 to 0.125
Outputs:
- grad_input: bfloat16 [8, 64, 16, 8, 128], P('dp', 'chan', 'space')
- grad_weight_one: float32 [128, 27, 64], P('chan')
- grad_weight_two: float32 [128, 27, 128], P('chan')
The draws below stay inside these ranges and needn't reach their ends.
All inputs are finite; a program needn't handle non-finite values.
Results may differ from the reference program's by a relative error of at most 0.0049.
Values may be sent and summed in bfloat16 or wider, within the bound.
No kernel may reach another device: no remote copies, remote signals or barrier semaphores. Data moves between devices by JAX's collectives and lax.ppermute only.
A program may use at most 64 MiB of HBM per device.

```python
import jax
import jax.numpy as jnp
from jax import lax

C0 = 64
C1 = 128
C2 = 128
BATCH = 8
NX = 16
NY = 8
NZ = 128


def strengthened(values, key, source, target, blocks, factor):
    def block_of(axis_at):
        return (jnp.arange(values.shape[axis_at]) // (values.shape[axis_at] // blocks)).reshape((-1,) + (1,) * (values.ndim - 1 - axis_at))

    first = jax.random.permutation(key, blocks)[block_of(target)]
    second = (block_of(target) + blocks // 2) % blocks
    return jnp.where((block_of(source) == first) | (block_of(source) == second), factor * values, values)


def block_levels(rng, extent, pieces, least, top_value):
    level = 1.0
    for dim, parts in pieces:
        heights = jax.random.uniform(jax.random.fold_in(jax.random.fold_in(rng, 6), dim), (parts,), jnp.float32, least / len(pieces), top_value / len(pieces))
        level = level * jnp.repeat(jnp.exp(heights), extent[dim] // parts).reshape((-1,) + (1,) * (len(extent) - 1 - dim))
    return level


def noise(rng, extent, scale, most, split=(), kind=jnp.bfloat16):
    result = jax.random.normal(rng, extent, jnp.float32) * scale
    if len(split) > 0:
        result = block_levels(rng, extent, split, -0.22, 0.18) * result
    return jnp.clip(result, min=-most, max=most).astype(kind)


def bell_draw_with(stream_key, shape, scale, limit, shards, heavy, dtype=jnp.bfloat16):
    drawn = scale * jax.random.normal(stream_key, shape, jnp.float32)
    if shards:
        drawn = drawn * block_levels(stream_key, shape, shards, -0.22, 0.18)
    return jnp.clip(strengthened(drawn, jax.random.fold_in(stream_key, 3), *heavy), -limit, limit).astype(dtype)


def setup_inputs(seed: int = 0) -> dict:
    key_of = jax.random.split(jax.random.key(seed), 7)
    return {
        "inputs": noise(key_of[0], (BATCH, C0, NX, NY, NZ), 1.0, 6.0, ((0, 8), (1, 4), (2, 8))),
        "pre_one": noise(key_of[1], (BATCH, C1, NX, NY, NZ), 1.0, 6.0, ((0, 8), (1, 4), (2, 8))),
        "pre_two": noise(key_of[2], (BATCH, C2, NX, NY, NZ), 1.0, 6.0, ((0, 8), (1, 4), (2, 8))),
        "grad_out": noise(key_of[3], (BATCH, C2, NX, NY, NZ), 1.0, 6.0, ((0, 8), (1, 4), (2, 8))),
        "weight_one": bell_draw_with(key_of[4], (C1, 27, C0), (27 * C0) ** -0.5, 0.21875, ((0, 4),), (0, 2, 4, 2.0)),
        "weight_two": bell_draw_with(key_of[5], (C2, 27, C1), (27 * C1) ** -0.5, 0.125, ((0, 4),), (0, 2, 4, 2.0)),
    }


def convolve(field, weights):
    kernel = weights.reshape(weights.shape[0], 3, 3, 3, weights.shape[2]).transpose(0, 4, 1, 2, 3)
    return lax.conv_general_dilated(field, kernel, (1, 1, 1), ((1, 1), (1, 1), (1, 1)), dimension_numbers=('NCDHW', 'OIDHW', 'NCDHW'), precision=lax.Precision.HIGHEST)

def reference(inputs, pre_one, pre_two, grad_out, weight_one, weight_two):
    delta_two = jnp.where(pre_two > 0, grad_out, jnp.zeros_like(grad_out))
    hidden = jnp.maximum(pre_one, jnp.zeros_like(pre_one))
    _, pull_two = jax.vjp(convolve, hidden.astype(jnp.float32), weight_two.astype(jnp.float32))
    hidden_grad, grad_weight_two = pull_two(delta_two.astype(jnp.float32))
    delta_one = jnp.where(pre_one > 0, hidden_grad, jnp.zeros_like(hidden_grad)).astype(jnp.bfloat16)
    _, pull_one = jax.vjp(convolve, inputs.astype(jnp.float32), weight_one.astype(jnp.float32))
    grad_input, grad_weight_one = pull_one(delta_one.astype(jnp.float32))
    return (grad_input.astype(jnp.bfloat16), grad_weight_one, grad_weight_two)
```

```python
import jax
import jax.numpy as jnp
from jax import lax
from jax.experimental import pallas as pl
from jax.experimental.pallas import tpu as pltpu
from jax.sharding import PartitionSpec as P

TAPS = 27
ROWS = 32
CELLS = 16
LANES = 128
DEPTH = TAPS * ROWS
CHUNK = 24
PARAMS = pltpu.CompilerParams(vmem_limit_bytes=40 * 1024 * 1024)


def fill_patches(patches, low, own, high):
    lane = lax.broadcasted_iota(jnp.int32, (ROWS, LANES), 1)
    first = lane == 0
    last = lane == LANES - 1
    empty = jnp.zeros((ROWS, LANES), jnp.bfloat16)

    def put(a, b, c, x, y, value):
        row = ((a * 3 + b) * 3 + c) * ROWS
        column = (x * 8 + y) * LANES
        patches[row : row + ROWS, column : column + LANES] = value

    for plane in range(4):
        for y in range(8):
            if plane == 0:
                block = low[y]
            elif plane == 3:
                block = high[y]
            else:
                block = own[(plane - 1) * 8 + y]
            wide = block.astype(jnp.float32)
            after = jnp.where(first, 0.0, pltpu.roll(wide, 1, 1)).astype(jnp.bfloat16)
            before = jnp.where(last, 0.0, pltpu.roll(wide, LANES - 1, 1)).astype(jnp.bfloat16)
            for c, value in enumerate((after, block, before)):
                for a in range(3):
                    x = plane - a
                    if x < 0 or x > 1:
                        continue
                    for b in range(3):
                        target = y + 1 - b
                        if 0 <= target < 8:
                            put(a, b, c, x, target, value)
    for a in range(3):
        for c in range(3):
            for x in range(2):
                put(a, 0, c, x, 0, empty)
                put(a, 2, c, x, 7, empty)


def data_two_kernel(low, own, high, weight, out, patches):
    fill_patches(patches, low, own, high)
    for group in range(4):
        columns = slice(group * 512, group * 512 + 512)
        result = jnp.dot(weight[...], patches[:, columns], preferred_element_type=jnp.float32)
        result = result.astype(jnp.bfloat16)
        for part in range(4):
            for cell in range(4):
                out[part, group * 4 + cell] = result[
                    part * 32 : part * 32 + 32, cell * LANES : cell * LANES + LANES
                ]


def lay_out(fields, source, start, count):
    for part in range(4):
        for cell in range(CELLS):
            fields[part * count : part * count + count, cell * LANES : cell * LANES + LANES] = source[
                part, cell, start : start + count
            ]


def tap_sums(patches, fields):
    sums = lax.dot_general(
        patches[...], fields[...], (((1,), (1,)), ((), ())), preferred_element_type=jnp.float32
    )
    return jnp.concatenate(
        [sums[(TAPS - 1 - k) * ROWS : (TAPS - k) * ROWS] for k in range(TAPS)], axis=0
    )


def filter_two_kernel(low, own, high, gathered, out, patches, fields):
    fill_patches(patches, low, own, high)
    lay_out(fields, gathered, 0, 32)
    out[...] = tap_sums(patches, fields).astype(jnp.bfloat16)


def layer_one_kernel(low, own, high, gathered, weight, filter_two, grad, sums, patches, fields):
    fill_patches(patches, low, own, high)
    lay_out(fields, gathered, 32, 16)
    for group in range(4):
        columns = slice(group * 512, group * 512 + 512)
        result = jnp.dot(weight[...], patches[:, columns], preferred_element_type=jnp.float32)
        for part in range(4):
            for cell in range(4):
                grad[part, group * 4 + cell] = result[
                    part * 16 : part * 16 + 16, cell * LANES : cell * LANES + LANES
                ]
    one = tap_sums(patches, fields)
    half = DEPTH // 2
    sums[0:DEPTH] = filter_two[...]
    sums[DEPTH : DEPTH + half] = jnp.concatenate([one[:half], one[half:]], axis=1).astype(jnp.bfloat16)
    sums[DEPTH + half :] = jnp.zeros((64 * CHUNK - DEPTH - half, LANES), jnp.bfloat16)


def call(kernel, outs, scratch, flops):
    return pl.pallas_call(
        kernel,
        out_shape=outs,
        scratch_shapes=scratch,
        compiler_params=PARAMS,
        cost_estimate=pl.CostEstimate(flops=flops, bytes_accessed=1 << 20, transcendentals=0),
    )


def by_rows(field):
    moved = field[0].transpose(1, 2, 0, 3)
    return moved.reshape((CELLS,) + moved.shape[2:])


def neighbours(field):
    count = lax.axis_size("space")
    forward = [(i, i + 1) for i in range(count - 1)]
    backward = [(i + 1, i) for i in range(count - 1)]
    low = lax.ppermute(field[8:], "space", forward)
    high = lax.ppermute(field[:8], "space", backward)
    return low, high


def flipped(weights):
    return weights[:, ::-1, :].transpose(2, 1, 0).reshape(weights.shape[2], DEPTH)


def local(inputs, pre_one, pre_two, grad_out, weight_one, weight_two):
    bf16 = jnp.bfloat16
    patches = pltpu.VMEM((DEPTH, CELLS * LANES), bf16)
    delta_two = by_rows(jnp.where(pre_two > 0, grad_out, jnp.zeros_like(grad_out)))
    low_two, high_two = neighbours(delta_two)
    pre_rows = by_rows(pre_one)
    hidden = jnp.maximum(pre_rows, jnp.zeros_like(pre_rows))
    both = jnp.concatenate([hidden, by_rows(inputs), jnp.zeros((CELLS, 16, LANES), bf16)], axis=1)
    gathered = lax.all_gather(both, "chan", axis=0, tiled=False)

    partial_two = call(
        data_two_kernel, jax.ShapeDtypeStruct((4, CELLS, 32, LANES), bf16), [patches], 500_000_000
    )(low_two, delta_two, high_two, flipped(weight_two))
    parts = lax.all_to_all(partial_two, "chan", 0, 0, tiled=True)
    hidden_grad = jnp.sum(parts.astype(jnp.float32), axis=0)
    delta_one = jnp.where(pre_rows > 0, hidden_grad, jnp.zeros_like(hidden_grad)).astype(bf16)
    low_one, high_one = neighbours(delta_one)

    filter_two = call(
        filter_two_kernel,
        jax.ShapeDtypeStruct((DEPTH, LANES), bf16),
        [patches, pltpu.VMEM((128, CELLS * LANES), bf16)],
        500_000_000,
    )(low_two, delta_two, high_two, gathered)

    grad, sums = call(
        layer_one_kernel,
        (
            jax.ShapeDtypeStruct((4, CELLS, 16, LANES), jnp.float32),
            jax.ShapeDtypeStruct((64 * CHUNK, LANES), bf16),
        ),
        [patches, pltpu.VMEM((64, CELLS * LANES), bf16)],
        500_000_000,
    )(low_one, delta_one, high_one, gathered, flipped(weight_one), filter_two)

    input_grad = lax.psum_scatter(grad, "chan", scatter_dimension=0, tiled=True)[0]
    input_grad = input_grad.reshape(2, 8, 16, LANES).transpose(2, 0, 1, 3)[None].astype(bf16)

    every = ("dp", "space")
    pieces = lax.all_to_all(sums.reshape(64, CHUNK, LANES), every, 0, 0, tiled=True)
    piece = jnp.sum(pieces.astype(jnp.float32), axis=0).astype(bf16)
    copies = jnp.broadcast_to(piece[None], (64, CHUNK, LANES))
    total = lax.all_to_all(copies, every, 0, 0, tiled=True).reshape(64 * CHUNK, LANES)
    total = total.astype(jnp.float32)
    half = DEPTH // 2
    grad_two = total[:DEPTH].reshape(TAPS, ROWS, LANES).transpose(1, 0, 2)
    one = total[DEPTH : DEPTH + half]
    one = jnp.concatenate([one[:, :64], one[:, 64:]], axis=0)
    grad_one = one.reshape(TAPS, ROWS, 64).transpose(1, 0, 2)
    return input_grad, grad_one, grad_two


def solution(mesh):
    field = P("dp", "chan", "space", None, None)
    weight = P("chan", None, None)
    return jax.shard_map(
        local,
        mesh=mesh,
        in_specs=(field, field, field, field, weight, weight),
        out_specs=(field, weight, weight),
        check_vma=False,
    )
```

```python
import jax
import jax.numpy as jnp
from jax import lax
from jax.experimental import pallas as pl
from jax.experimental.pallas import tpu as pltpu
from jax.sharding import PartitionSpec as P

TAPS = 27
ROWS = 32
CELLS = 16
LANES = 128
DEPTH = TAPS * ROWS
CHUNK = 24
PARAMS = pltpu.CompilerParams(vmem_limit_bytes=14 * 1024 * 1024)


def fill_patches(patches, low, own, high):
    lane = lax.broadcasted_iota(jnp.int32, (ROWS, LANES), 1)
    first = lane == 0
    last = lane == LANES - 1
    empty = jnp.zeros((ROWS, LANES), jnp.bfloat16)

    def put(a, b, c, x, y, value):
        row = ((a * 3 + b) * 3 + c) * ROWS
        column = (x * 8 + y) * LANES
        patches[row : row + ROWS, column : column + LANES] = value

    for plane in range(4):
        for y in range(8):
            if plane == 0:
                block = low[y]
            elif plane == 3:
                block = high[y]
            else:
                block = own[(plane - 1) * 8 + y]
            wide = block.astype(jnp.float32)
            after = jnp.where(first, 0.0, pltpu.roll(wide, 1, 1)).astype(jnp.bfloat16)
            before = jnp.where(last, 0.0, pltpu.roll(wide, LANES - 1, 1)).astype(jnp.bfloat16)
            for c, value in enumerate((after, block, before)):
                for a in range(3):
                    x = plane - a
                    if x < 0 or x > 1:
                        continue
                    for b in range(3):
                        target = y + 1 - b
                        if 0 <= target < 8:
                            put(a, b, c, x, target, value)
    for a in range(3):
        for c in range(3):
            for x in range(2):
                put(a, 0, c, x, 0, empty)
                put(a, 2, c, x, 7, empty)


def data_two_kernel(low, own, high, weight, out, patches):
    fill_patches(patches, low, own, high)
    for group in range(4):
        columns = slice(group * 512, group * 512 + 512)
        result = jnp.dot(weight[...], patches[:, columns], preferred_element_type=jnp.float32)
        result = result.astype(jnp.bfloat16)
        for part in range(4):
            for cell in range(4):
                out[part, group * 4 + cell] = result[
                    part * 32 : part * 32 + 32, cell * LANES : cell * LANES + LANES
                ]


def lay_out(fields, me, blocks, start, count):
    own, left, right, far_first, far_second = blocks
    for shift in range(4):
        part = lax.rem(me[0] + shift, 4)
        rows = pl.ds(pl.multiple_of(part * count, count), count)
        for cell in range(CELLS):
            if shift == 2:
                source = far_first[cell] if cell < 8 else far_second[cell - 8]
            else:
                source = (own, right, None, left)[shift][cell]
            fields[rows, cell * LANES : cell * LANES + LANES] = source[start : start + count]


def tap_sums(patches, fields):
    sums = lax.dot_general(
        patches[...], fields[...], (((1,), (1,)), ((), ())), preferred_element_type=jnp.float32
    )
    return jnp.concatenate(
        [sums[(TAPS - 1 - k) * ROWS : (TAPS - k) * ROWS] for k in range(TAPS)], axis=0
    )


def filter_two_kernel(me, low, own, high, b0, b1, b2, b3, b4, out, patches, fields):
    fill_patches(patches, low, own, high)
    lay_out(fields, me, (b0, b1, b2, b3, b4), 0, 32)
    out[...] = tap_sums(patches, fields).astype(jnp.bfloat16)


def pack_kernel(b0, b1, b2, b3, b4, first, second):
    for y in range(8):
        for shift, source in enumerate((b0, b2, b3, b1)):
            first[y, shift * 16 : shift * 16 + 16] = source[y, 32:48]
        for shift, source in enumerate((b0, b2, b4, b1)):
            second[y, shift * 16 : shift * 16 + 16] = source[y if shift == 2 else 8 + y, 32:48]


def filter_one_kernel(
    me, parts, b0, b1, b2, b3, b4, in_low, in_high, filter_two, delta, sums, shifted, fields
):
    lane = lax.broadcasted_iota(jnp.int32, (ROWS, LANES), 1)
    for cell in range(CELLS):
        total = parts[0, cell].astype(jnp.float32)
        for part in range(1, 4):
            total = total + parts[part, cell].astype(jnp.float32)
        total = jnp.where(b0[cell, 0:ROWS].astype(jnp.float32) > 0, total, 0.0)
        block = total.astype(jnp.bfloat16)
        delta[cell] = block
        wide = block.astype(jnp.float32)
        before = jnp.where(lane == LANES - 1, 0.0, pltpu.roll(wide, LANES - 1, 1))
        after = jnp.where(lane == 0, 0.0, pltpu.roll(wide, 1, 1))
        column = cell * LANES
        shifted[0:ROWS, column : column + LANES] = before.astype(jnp.bfloat16)
        shifted[ROWS : 2 * ROWS, column : column + LANES] = block
        shifted[2 * ROWS : 3 * ROWS, column : column + LANES] = after.astype(jnp.bfloat16)
    for shift in range(4):
        part = lax.rem(me[0] + shift, 4)
        rows = pl.ds(pl.multiple_of(part * 16, 16), 16)
        for plane in range(4):
            for y in range(8):
                if plane == 0:
                    value = in_low[y, shift * 16 : shift * 16 + 16]
                elif plane == 3:
                    value = in_high[y, shift * 16 : shift * 16 + 16]
                elif shift == 2:
                    value = (b3, b4)[plane - 1][y, 32:48]
                else:
                    value = (b0, b2, None, b1)[shift][(plane - 1) * 8 + y, 32:48]
                column = (plane * 10 + y + 1) * LANES
                fields[rows, column : column + LANES] = value
    empty = jnp.zeros((64, LANES), jnp.bfloat16)
    for plane in range(4):
        for y in (0, 9):
            column = (plane * 10 + y) * LANES
            fields[:, column : column + LANES] = empty
    taps = []
    for a in range(3):
        for b in range(3):
            total = None
            for x in range(2):
                column = ((x + a) * 10 + b) * LANES
                term = lax.dot_general(
                    shifted[:, x * 1024 : x * 1024 + 1024],
                    fields[:, column : column + 1024],
                    (((1,), (1,)), ((), ())),
                    preferred_element_type=jnp.float32,
                )
                total = term if total is None else total + term
            taps.append(total)
    one = jnp.concatenate(taps, axis=0)
    half = DEPTH // 2
    sums[0:DEPTH] = filter_two[...]
    sums[DEPTH : DEPTH + half] = jnp.concatenate([one[:half], one[half:]], axis=1).astype(jnp.bfloat16)
    sums[DEPTH + half :] = jnp.zeros((64 * CHUNK - DEPTH - half, LANES), jnp.bfloat16)


def data_one_kernel(low, own, high, weight, keep, right, across, left, patches):
    fill_patches(patches, low, own, high)
    for group in range(4):
        columns = slice(group * 512, group * 512 + 512)
        result = jnp.dot(weight[...], patches[:, columns], preferred_element_type=jnp.float32)
        for part, target in enumerate((keep, right, across, left)):
            for cell in range(4):
                target[group * 4 + cell] = result[
                    part * 16 : part * 16 + 16, cell * LANES : cell * LANES + LANES
                ].astype(target.dtype)


def add_kernel(pieces, copies):
    total = pieces[0].astype(jnp.float32)
    for index in range(1, 64):
        total = total + pieces[index].astype(jnp.float32)
    total = total.astype(jnp.bfloat16)
    for index in range(64):
        copies[index] = total


def unpack_kernel(rows, two, one):
    two[...] = rows[0:DEPTH].astype(jnp.float32)
    half = DEPTH // 2
    pairs = rows[DEPTH : DEPTH + half].astype(jnp.float32)
    one[0:half] = pairs[:, 0:64]
    one[half:] = pairs[:, 64:128]


def call(kernel, outs, scratch, flops, arrays, scalars=0):
    memory = pl.BlockSpec(memory_space=pltpu.SMEM)
    return pl.pallas_call(
        kernel,
        out_shape=outs,
        in_specs=[memory] * scalars + [pl.BlockSpec(memory_space=pltpu.VMEM)] * arrays,
        scratch_shapes=scratch,
        compiler_params=PARAMS,
        cost_estimate=pl.CostEstimate(flops=flops, bytes_accessed=1 << 20, transcendentals=0),
    )


def by_rows(field):
    moved = field[0].transpose(1, 2, 0, 3)
    return moved.reshape((CELLS,) + moved.shape[2:])


def neighbours(first, second):
    count = lax.axis_size("space")
    forward = [(i, i + 1) for i in range(count - 1)]
    backward = [(i + 1, i) for i in range(count - 1)]
    low = lax.ppermute(second, "space", forward)
    high = lax.ppermute(first, "space", backward)
    return low, high


def flipped(weights):
    return weights[:, ::-1, :].transpose(2, 1, 0).reshape(weights.shape[2], DEPTH)


def from_this(weights, me, count):
    rows = flipped(weights)
    return lax.dynamic_slice_in_dim(jnp.concatenate([rows, rows], axis=0), me * count, 4 * count, axis=0)


def over_chan(keep, right, across, left):
    ring = lambda step: [(i, (i + step) % 4) for i in range(4)]
    across = lax.ppermute(across, "chan", ring(2))
    right = lax.ppermute(right, "chan", ring(1))
    left = lax.ppermute(left, "chan", ring(3))
    return keep, right, across, left


def shares(count):
    shape = (CELLS, count, LANES)
    return (jax.ShapeDtypeStruct(shape, jnp.float32),) + (jax.ShapeDtypeStruct(shape, jnp.bfloat16),) * 3


def local(inputs, pre_one, pre_two, grad_out, weight_one, weight_two):
    bf16 = jnp.bfloat16
    patches = pltpu.VMEM((DEPTH, CELLS * LANES), bf16)
    delta_two = by_rows(jnp.where(pre_two > 0, grad_out, jnp.zeros_like(grad_out)))
    low_two, high_two = neighbours(delta_two[:8], delta_two[8:])
    hidden = by_rows(jnp.maximum(pre_one, jnp.zeros_like(pre_one)))
    both = jnp.concatenate([hidden, by_rows(inputs)], axis=1)
    to_right = [(i, (i + 1) % 4) for i in range(4)]
    to_left = [(i, (i + 3) % 4) for i in range(4)]
    from_left = lax.ppermute(both, "chan", to_right)
    from_right = lax.ppermute(both, "chan", to_left)
    me = lax.axis_index("chan").astype(jnp.int32)

    partial_two = call(
        data_two_kernel, jax.ShapeDtypeStruct((4, CELLS, 32, LANES), bf16), [patches], 2_500_000_000, 4
    )(low_two, delta_two, high_two, flipped(weight_two))
    partial_two, from_left, from_right = lax.optimization_barrier((partial_two, from_left, from_right))
    parts = lax.all_to_all(partial_two, "chan", 0, 0, tiled=True)

    far_first = lax.ppermute(from_left[:8], "chan", to_right)
    far_second = lax.ppermute(from_right[8:], "chan", to_left)
    blocks = (both, from_left, from_right, far_first, far_second)
    plane = jax.ShapeDtypeStruct((8, 64, LANES), bf16)
    first, second = call(pack_kernel, (plane, plane), [], 8_000_000_000, 5)(*blocks)
    in_low, in_high = neighbours(first, second)
    filter_two = call(
        filter_two_kernel,
        jax.ShapeDtypeStruct((DEPTH, LANES), bf16),
        [patches, pltpu.VMEM((128, CELLS * LANES), bf16)],
        500_000_000,
        8,
        1,
    )(me[None], low_two, delta_two, high_two, *blocks)

    parts, in_low, in_high, filter_two = lax.optimization_barrier((parts, in_low, in_high, filter_two))
    delta_one, sums = call(
        filter_one_kernel,
        (
            jax.ShapeDtypeStruct((CELLS, ROWS, LANES), bf16),
            jax.ShapeDtypeStruct((64 * CHUNK, LANES), bf16),
        ),
        [pltpu.VMEM((3 * ROWS, CELLS * LANES), bf16), pltpu.VMEM((64, 40 * LANES), bf16)],
        500_000_000,
        9,
        1,
    )(me[None], parts, *blocks, in_low, in_high, filter_two)

    every = ("dp", "space")
    pieces = lax.all_to_all(sums.reshape(64, CHUNK, LANES), every, 0, 0, tiled=True)
    low_one, high_one = neighbours(delta_one[:8], delta_one[8:])
    partial_one = call(data_one_kernel, shares(16), [patches], 500_000_000, 4)(
        low_one, delta_one, high_one, from_this(weight_one, me, 16)
    )
    pieces, partial_one = lax.optimization_barrier((pieces, partial_one))
    copies = call(add_kernel, jax.ShapeDtypeStruct((64, CHUNK, LANES), bf16), [], 0, 1)(pieces)
    keep, right, across, left = over_chan(*partial_one)
    input_grad = keep + right.astype(jnp.float32) + across.astype(jnp.float32) + left.astype(jnp.float32)
    input_grad = input_grad.astype(bf16).reshape(2, 8, 16, LANES).transpose(2, 0, 1, 3)[None]
    total = lax.all_to_all(copies, every, 0, 0, tiled=True).reshape(64 * CHUNK, LANES)
    two, one = call(
        unpack_kernel,
        (jax.ShapeDtypeStruct((DEPTH, LANES), jnp.float32), jax.ShapeDtypeStruct((DEPTH, 64), jnp.float32)),
        [],
        0,
        1,
    )(total)
    grad_two = two.reshape(TAPS, ROWS, LANES).transpose(1, 0, 2)
    grad_one = one.reshape(TAPS, ROWS, 64).transpose(1, 0, 2)
    return input_grad, grad_one, grad_two


def solution(mesh):
    field = P("dp", "chan", "space", None, None)
    weight = P("chan", None, None)
    return jax.shard_map(
        local,
        mesh=mesh,
        in_specs=(field, field, field, field, weight, weight),
        out_specs=(field, weight, weight),
        check_vma=False,
    )
```

```python
import jax
import jax.numpy as jnp
from jax import lax
from jax.experimental import pallas as pl
from jax.experimental.pallas import tpu as pltpu
from jax.sharding import PartitionSpec as P

TAPS = 27
ROWS = 32
CELLS = 16
LANES = 128
DEPTH = TAPS * ROWS
CHUNK = 24
PARAMS = pltpu.CompilerParams(vmem_limit_bytes=14 * 1024 * 1024)


def fill_patches(patches, low, own, high):
    lane = lax.broadcasted_iota(jnp.int32, (ROWS, LANES), 1)
    first = lane == 0
    last = lane == LANES - 1
    empty = jnp.zeros((ROWS, LANES), jnp.bfloat16)

    def put(a, b, c, x, y, value):
        row = ((a * 3 + b) * 3 + c) * ROWS
        column = (x * 8 + y) * LANES
        patches[row : row + ROWS, column : column + LANES] = value

    for plane in range(4):
        for y in range(8):
            if plane == 0:
                block = low[y]
            elif plane == 3:
                block = high[y]
            else:
                block = own[(plane - 1) * 8 + y]
            wide = block.astype(jnp.float32)
            after = jnp.where(first, 0.0, pltpu.roll(wide, 1, 1)).astype(jnp.bfloat16)
            before = jnp.where(last, 0.0, pltpu.roll(wide, LANES - 1, 1)).astype(jnp.bfloat16)
            for c, value in enumerate((after, block, before)):
                for a in range(3):
                    x = plane - a
                    if x < 0 or x > 1:
                        continue
                    for b in range(3):
                        target = y + 1 - b
                        if 0 <= target < 8:
                            put(a, b, c, x, target, value)
    for a in range(3):
        for c in range(3):
            for x in range(2):
                put(a, 0, c, x, 0, empty)
                put(a, 2, c, x, 7, empty)


def data_two_kernel(low, own, high, weight, out, patches):
    fill_patches(patches, low, own, high)
    for group in range(4):
        columns = slice(group * 512, group * 512 + 512)
        result = jnp.dot(weight[...], patches[:, columns], preferred_element_type=jnp.float32)
        result = result.astype(jnp.bfloat16)
        for part in range(4):
            for cell in range(4):
                out[part, group * 4 + cell] = result[
                    part * 32 : part * 32 + 32, cell * LANES : cell * LANES + LANES
                ]


def lay_out(fields, me, blocks, start, count):
    own, left, right, far_first, far_second = blocks
    for shift in range(4):
        part = lax.rem(me[0] + shift, 4)
        rows = pl.ds(pl.multiple_of(part * count, count), count)
        for cell in range(CELLS):
            if shift == 2:
                source = far_first[cell] if cell < 8 else far_second[cell - 8]
            else:
                source = (own, right, None, left)[shift][cell]
            fields[rows, cell * LANES : cell * LANES + LANES] = source[start : start + count]


def tap_sums(patches, fields):
    sums = lax.dot_general(
        patches[...], fields[...], (((1,), (1,)), ((), ())), preferred_element_type=jnp.float32
    )
    return jnp.concatenate(
        [sums[(TAPS - 1 - k) * ROWS : (TAPS - k) * ROWS] for k in range(TAPS)], axis=0
    )


def filter_two_kernel(me, low, own, high, b0, b1, b2, b3, b4, out, patches, fields):
    fill_patches(patches, low, own, high)
    lay_out(fields, me, (b0, b1, b2, b3, b4), 0, 32)
    out[...] = tap_sums(patches, fields).astype(jnp.bfloat16)


def pass_kernel(from_left, from_right, first, second):
    first[...] = from_left[0:8]
    second[...] = from_right[8:16]


def filter_one_kernel(me, low, own, high, b0, b1, b2, b3, b4, filter_two, sums, patches, fields):
    fill_patches(patches, low, own, high)
    lay_out(fields, me, (b0, b1, b2, b3, b4), 32, 16)
    one = tap_sums(patches, fields)
    half = DEPTH // 2
    sums[0:DEPTH] = filter_two[...]
    sums[DEPTH : DEPTH + half] = jnp.concatenate([one[:half], one[half:]], axis=1).astype(jnp.bfloat16)
    sums[DEPTH + half :] = jnp.zeros((64 * CHUNK - DEPTH - half, LANES), jnp.bfloat16)


def data_one_kernel(low, own, high, weight, keep, right, across, left, patches):
    fill_patches(patches, low, own, high)
    for group in range(4):
        columns = slice(group * 512, group * 512 + 512)
        result = jnp.dot(weight[...], patches[:, columns], preferred_element_type=jnp.float32)
        for part, target in enumerate((keep, right, across, left)):
            for cell in range(4):
                target[group * 4 + cell] = result[
                    part * 16 : part * 16 + 16, cell * LANES : cell * LANES + LANES
                ].astype(target.dtype)


def add_kernel(pieces, copies):
    total = pieces[0].astype(jnp.float32)
    for index in range(1, 64):
        total = total + pieces[index].astype(jnp.float32)
    total = total.astype(jnp.bfloat16)
    for index in range(64):
        copies[index] = total


def unpack_kernel(rows, two, one):
    two[...] = rows[0:DEPTH].astype(jnp.float32)
    half = DEPTH // 2
    pairs = rows[DEPTH : DEPTH + half].astype(jnp.float32)
    one[0:half] = pairs[:, 0:64]
    one[half:] = pairs[:, 64:128]


def call(kernel, outs, scratch, flops, arrays, scalars=0):
    memory = pl.BlockSpec(memory_space=pltpu.SMEM)
    return pl.pallas_call(
        kernel,
        out_shape=outs,
        in_specs=[memory] * scalars + [pl.BlockSpec(memory_space=pltpu.VMEM)] * arrays,
        scratch_shapes=scratch,
        compiler_params=PARAMS,
        cost_estimate=pl.CostEstimate(flops=flops, bytes_accessed=1 << 20, transcendentals=0),
    )


def by_rows(field):
    moved = field[0].transpose(1, 2, 0, 3)
    return moved.reshape((CELLS,) + moved.shape[2:])


def neighbours(first, second):
    count = lax.axis_size("space")
    forward = [(i, i + 1) for i in range(count - 1)]
    backward = [(i + 1, i) for i in range(count - 1)]
    low = lax.ppermute(second, "space", forward)
    high = lax.ppermute(first, "space", backward)
    return low, high


def flipped(weights):
    return weights[:, ::-1, :].transpose(2, 1, 0).reshape(weights.shape[2], DEPTH)


def from_this(weights, me, count):
    rows = flipped(weights)
    return lax.dynamic_slice_in_dim(jnp.concatenate([rows, rows], axis=0), me * count, 4 * count, axis=0)


def shares(count):
    shape = (CELLS, count, LANES)
    return (jax.ShapeDtypeStruct(shape, jnp.float32),) + (jax.ShapeDtypeStruct(shape, jnp.bfloat16),) * 3


def local(inputs, pre_one, pre_two, grad_out, weight_one, weight_two):
    bf16 = jnp.bfloat16
    patches = pltpu.VMEM((DEPTH, CELLS * LANES), bf16)
    delta_two = by_rows(jnp.where(pre_two > 0, grad_out, jnp.zeros_like(grad_out)))
    low_two, high_two = neighbours(delta_two[:8], delta_two[8:])
    hidden = by_rows(jnp.maximum(pre_one, jnp.zeros_like(pre_one)))
    both = jnp.concatenate([hidden, by_rows(inputs)], axis=1)
    to_right = [(i, (i + 1) % 4) for i in range(4)]
    to_left = [(i, (i + 3) % 4) for i in range(4)]
    from_left = lax.ppermute(both, "chan", to_right)
    from_right = lax.ppermute(both, "chan", to_left)
    me = lax.axis_index("chan").astype(jnp.int32)

    partial_two = call(
        data_two_kernel, jax.ShapeDtypeStruct((4, CELLS, 32, LANES), bf16), [patches], 2_500_000_000, 4
    )(low_two, delta_two, high_two, flipped(weight_two))
    parts = lax.all_to_all(partial_two, "chan", 0, 0, tiled=True)

    halves = call(pass_kernel, (jax.ShapeDtypeStruct((8, 48, LANES), bf16),) * 2, [], 11_000_000_000, 2)(
        from_left, from_right
    )
    far_first = lax.ppermute(halves[0], "chan", to_right)
    far_second = lax.ppermute(halves[1], "chan", to_left)
    blocks = (both, from_left, from_right, far_first, far_second)

    hidden_grad = jnp.sum(parts.astype(jnp.float32), axis=0)
    delta_one = jnp.where(hidden > 0, hidden_grad, jnp.zeros_like(hidden_grad)).astype(bf16)
    low_one, high_one = neighbours(delta_one[:8], delta_one[8:])
    filter_two = call(
        filter_two_kernel,
        jax.ShapeDtypeStruct((DEPTH, LANES), bf16),
        [patches, pltpu.VMEM((128, CELLS * LANES), bf16)],
        500_000_000,
        8,
        1,
    )(me[None], low_two, delta_two, high_two, *blocks)

    sums = call(
        filter_one_kernel,
        jax.ShapeDtypeStruct((64 * CHUNK, LANES), bf16),
        [patches, pltpu.VMEM((64, CELLS * LANES), bf16)],
        500_000_000,
        9,
        1,
    )(me[None], low_one, delta_one, high_one, *blocks, filter_two)

    every = ("dp", "space")
    sums, low_one, high_one = lax.optimization_barrier((sums, low_one, high_one))
    pieces = lax.all_to_all(sums.reshape(64, CHUNK, LANES), every, 0, 0, tiled=True)
    pieces, low_one, high_one = lax.optimization_barrier((pieces, low_one, high_one))
    copies = call(add_kernel, jax.ShapeDtypeStruct((64, CHUNK, LANES), bf16), [], 0, 1)(pieces)
    partial_one = call(data_one_kernel, shares(16), [patches], 500_000_000, 4)(
        low_one, delta_one, high_one, from_this(weight_one, me, 16)
    )
    keep, right, across, left = partial_one
    across = lax.ppermute(across, "chan", [(i, (i + 2) % 4) for i in range(4)])
    right = lax.ppermute(right, "chan", to_right)
    left = lax.ppermute(left, "chan", to_left)
    input_grad = keep + right.astype(jnp.float32) + across.astype(jnp.float32) + left.astype(jnp.float32)
    input_grad = input_grad.astype(bf16).reshape(2, 8, 16, LANES).transpose(2, 0, 1, 3)[None]
    total = lax.all_to_all(copies, every, 0, 0, tiled=True).reshape(64 * CHUNK, LANES)
    two, one = call(
        unpack_kernel,
        (jax.ShapeDtypeStruct((DEPTH, LANES), jnp.float32), jax.ShapeDtypeStruct((DEPTH, 64), jnp.float32)),
        [],
        0,
        1,
    )(total)
    grad_two = two.reshape(TAPS, ROWS, LANES).transpose(1, 0, 2)
    grad_one = one.reshape(TAPS, ROWS, 64).transpose(1, 0, 2)
    return input_grad, grad_one, grad_two


def solution(mesh):
    field = P("dp", "chan", "space", None, None)
    weight = P("chan", None, None)
    return jax.shard_map(
        local,
        mesh=mesh,
        in_specs=(field, field, field, field, weight, weight),
        out_specs=(field, weight, weight),
        check_vma=False,
    )
```

```python
import jax
import jax.numpy as jnp
from jax import lax
from jax.experimental import pallas as pl
from jax.experimental.pallas import tpu as pltpu
from jax.sharding import PartitionSpec as P

TAPS = 27
ROWS = 32
CELLS = 16
LANES = 128
DEPTH = TAPS * ROWS
CHUNK = 24
PARAMS = pltpu.CompilerParams(vmem_limit_bytes=14 * 1024 * 1024)


def fill_patches(patches, low, own, high):
    lane = lax.broadcasted_iota(jnp.int32, (ROWS, LANES), 1)
    first = lane == 0
    last = lane == LANES - 1
    empty = jnp.zeros((ROWS, LANES), jnp.bfloat16)

    def put(a, b, c, x, y, value):
        row = ((a * 3 + b) * 3 + c) * ROWS
        column = (x * 8 + y) * LANES
        patches[row : row + ROWS, column : column + LANES] = value

    for plane in range(4):
        for y in range(8):
            if plane == 0:
                block = low[y]
            elif plane == 3:
                block = high[y]
            else:
                block = own[(plane - 1) * 8 + y]
            wide = block.astype(jnp.float32)
            after = jnp.where(first, 0.0, pltpu.roll(wide, 1, 1)).astype(jnp.bfloat16)
            before = jnp.where(last, 0.0, pltpu.roll(wide, LANES - 1, 1)).astype(jnp.bfloat16)
            for c, value in enumerate((after, block, before)):
                for a in range(3):
                    x = plane - a
                    if x < 0 or x > 1:
                        continue
                    for b in range(3):
                        target = y + 1 - b
                        if 0 <= target < 8:
                            put(a, b, c, x, target, value)
    for a in range(3):
        for c in range(3):
            for x in range(2):
                put(a, 0, c, x, 0, empty)
                put(a, 2, c, x, 7, empty)


def data_two_kernel(low, own, high, weight, out, patches):
    fill_patches(patches, low, own, high)
    for group in range(4):
        columns = slice(group * 512, group * 512 + 512)
        result = jnp.dot(weight[...], patches[:, columns], preferred_element_type=jnp.float32)
        result = result.astype(jnp.bfloat16)
        for part in range(4):
            for cell in range(4):
                out[part, group * 4 + cell] = result[
                    part * 32 : part * 32 + 32, cell * LANES : cell * LANES + LANES
                ]


def lay_out(fields, me, blocks, start, count):
    own, left, right, far_first, far_second = blocks
    for shift in range(4):
        part = lax.rem(me[0] + shift, 4)
        rows = pl.ds(pl.multiple_of(part * count, count), count)
        for cell in range(CELLS):
            if shift == 2:
                source = far_first[cell] if cell < 8 else far_second[cell - 8]
            else:
                source = (own, right, None, left)[shift][cell]
            fields[rows, cell * LANES : cell * LANES + LANES] = source[start : start + count]


def tap_sums(patches, fields):
    sums = lax.dot_general(
        patches[...], fields[...], (((1,), (1,)), ((), ())), preferred_element_type=jnp.float32
    )
    return jnp.concatenate(
        [sums[(TAPS - 1 - k) * ROWS : (TAPS - k) * ROWS] for k in range(TAPS)], axis=0
    )


def filter_two_kernel(me, low, own, high, b0, b1, b2, b3, b4, out, patches, fields):
    fill_patches(patches, low, own, high)
    lay_out(fields, me, (b0, b1, b2, b3, b4), 0, 32)
    out[...] = tap_sums(patches, fields).astype(jnp.bfloat16)


def pass_kernel(from_left, from_right, first, second):
    first[...] = from_left[0:8]
    second[...] = from_right[8:16]


def filter_one_kernel(me, low, own, high, b0, b1, b2, b3, b4, filter_two, sums, patches, fields):
    fill_patches(patches, low, own, high)
    lay_out(fields, me, (b0, b1, b2, b3, b4), 32, 16)
    one = tap_sums(patches, fields)
    half = DEPTH // 2
    sums[0:DEPTH] = filter_two[...]
    sums[DEPTH : DEPTH + half] = jnp.concatenate([one[:half], one[half:]], axis=1).astype(jnp.bfloat16)
    sums[DEPTH + half :] = jnp.zeros((64 * CHUNK - DEPTH - half, LANES), jnp.bfloat16)


def data_one_kernel(low, own, high, weight, keep, right, across, left, patches):
    fill_patches(patches, low, own, high)
    for group in range(4):
        columns = slice(group * 512, group * 512 + 512)
        result = jnp.dot(weight[...], patches[:, columns], preferred_element_type=jnp.float32)
        for part, target in enumerate((keep, right, across, left)):
            for cell in range(4):
                target[group * 4 + cell] = result[
                    part * 16 : part * 16 + 16, cell * LANES : cell * LANES + LANES
                ].astype(target.dtype)


def add_kernel(pieces, copies):
    total = pieces[0].astype(jnp.float32)
    for index in range(1, 64):
        total = total + pieces[index].astype(jnp.float32)
    total = total.astype(jnp.bfloat16)
    for index in range(64):
        copies[index] = total


def unpack_kernel(rows, two, one):
    two[...] = rows[0:DEPTH].astype(jnp.float32)
    half = DEPTH // 2
    pairs = rows[DEPTH : DEPTH + half].astype(jnp.float32)
    one[0:half] = pairs[:, 0:64]
    one[half:] = pairs[:, 64:128]


def call(kernel, outs, scratch, flops, arrays, scalars=0):
    memory = pl.BlockSpec(memory_space=pltpu.SMEM)
    return pl.pallas_call(
        kernel,
        out_shape=outs,
        in_specs=[memory] * scalars + [pl.BlockSpec(memory_space=pltpu.VMEM)] * arrays,
        scratch_shapes=scratch,
        compiler_params=PARAMS,
        cost_estimate=pl.CostEstimate(flops=flops, bytes_accessed=1 << 20, transcendentals=0),
    )


def by_rows(field):
    moved = field[0].transpose(1, 2, 0, 3)
    return moved.reshape((CELLS,) + moved.shape[2:])


def neighbours(first, second):
    count = lax.axis_size("space")
    forward = [(i, i + 1) for i in range(count - 1)]
    backward = [(i + 1, i) for i in range(count - 1)]
    low = lax.ppermute(second, "space", forward)
    high = lax.ppermute(first, "space", backward)
    return low, high


def flipped(weights):
    return weights[:, ::-1, :].transpose(2, 1, 0).reshape(weights.shape[2], DEPTH)


def from_this(weights, me, count):
    rows = flipped(weights)
    return lax.dynamic_slice_in_dim(jnp.concatenate([rows, rows], axis=0), me * count, 4 * count, axis=0)


def shares(count):
    shape = (CELLS, count, LANES)
    return (jax.ShapeDtypeStruct(shape, jnp.float32),) + (jax.ShapeDtypeStruct(shape, jnp.bfloat16),) * 3


def local(inputs, pre_one, pre_two, grad_out, weight_one, weight_two):
    bf16 = jnp.bfloat16
    patches = pltpu.VMEM((DEPTH, CELLS * LANES), bf16)
    delta_two = by_rows(jnp.where(pre_two > 0, grad_out, jnp.zeros_like(grad_out)))
    low_two, high_two = neighbours(delta_two[:8], delta_two[8:])
    hidden = by_rows(jnp.maximum(pre_one, jnp.zeros_like(pre_one)))
    both = jnp.concatenate([hidden, by_rows(inputs)], axis=1)
    to_right = [(i, (i + 1) % 4) for i in range(4)]
    to_left = [(i, (i + 3) % 4) for i in range(4)]
    from_left = lax.ppermute(both, "chan", to_right)
    from_right = lax.ppermute(both, "chan", to_left)
    me = lax.axis_index("chan").astype(jnp.int32)

    partial_two = call(
        data_two_kernel, jax.ShapeDtypeStruct((4, CELLS, 32, LANES), bf16), [patches], 2_500_000_000, 4
    )(low_two, delta_two, high_two, flipped(weight_two))
    parts = lax.all_to_all(partial_two, "chan", 0, 0, tiled=True)

    halves = call(pass_kernel, (jax.ShapeDtypeStruct((8, 48, LANES), bf16),) * 2, [], 15_500_000_000, 2)(
        from_left, from_right
    )
    hidden_grad = jnp.sum(parts.astype(jnp.float32), axis=0)
    delta_one = jnp.where(hidden > 0, hidden_grad, jnp.zeros_like(hidden_grad)).astype(bf16)
    first_half, second_half, delta_one = lax.optimization_barrier((*halves, delta_one))
    far_first = lax.ppermute(first_half, "chan", to_right)
    far_second = lax.ppermute(second_half, "chan", to_left)
    blocks = (both, from_left, from_right, far_first, far_second)

    low_one, high_one = neighbours(delta_one[:8], delta_one[8:])
    filter_two = call(
        filter_two_kernel,
        jax.ShapeDtypeStruct((DEPTH, LANES), bf16),
        [patches, pltpu.VMEM((128, CELLS * LANES), bf16)],
        500_000_000,
        8,
        1,
    )(me[None], low_two, delta_two, high_two, *blocks)

    sums = call(
        filter_one_kernel,
        jax.ShapeDtypeStruct((64 * CHUNK, LANES), bf16),
        [patches, pltpu.VMEM((64, CELLS * LANES), bf16)],
        500_000_000,
        9,
        1,
    )(me[None], low_one, delta_one, high_one, *blocks, filter_two)

    every = ("dp", "space")
    sums, low_one, high_one = lax.optimization_barrier((sums, low_one, high_one))
    pieces = lax.all_to_all(sums.reshape(64, CHUNK, LANES), every, 0, 0, tiled=True)
    pieces, low_one, high_one = lax.optimization_barrier((pieces, low_one, high_one))
    copies = call(add_kernel, jax.ShapeDtypeStruct((64, CHUNK, LANES), bf16), [], 0, 1)(pieces)
    partial_one = call(data_one_kernel, shares(16), [patches], 500_000_000, 4)(
        low_one, delta_one, high_one, from_this(weight_one, me, 16)
    )
    keep, right, across, left = partial_one
    across = lax.ppermute(across, "chan", [(i, (i + 2) % 4) for i in range(4)])
    right = lax.ppermute(right, "chan", to_right)
    left = lax.ppermute(left, "chan", to_left)
    input_grad = keep + right.astype(jnp.float32) + across.astype(jnp.float32) + left.astype(jnp.float32)
    input_grad = input_grad.astype(bf16).reshape(2, 8, 16, LANES).transpose(2, 0, 1, 3)[None]
    total = lax.all_to_all(copies, every, 0, 0, tiled=True).reshape(64 * CHUNK, LANES)
    two, one = call(
        unpack_kernel,
        (jax.ShapeDtypeStruct((DEPTH, LANES), jnp.float32), jax.ShapeDtypeStruct((DEPTH, 64), jnp.float32)),
        [],
        0,
        1,
    )(total)
    grad_two = two.reshape(TAPS, ROWS, LANES).transpose(1, 0, 2)
    grad_one = one.reshape(TAPS, ROWS, 64).transpose(1, 0, 2)
    return input_grad, grad_one, grad_two


def solution(mesh):
    field = P("dp", "chan", "space", None, None)
    weight = P("chan", None, None)
    return jax.shard_map(
        local,
        mesh=mesh,
        in_specs=(field, field, field, field, weight, weight),
        out_specs=(field, weight, weight),
        check_vma=False,
    )
```
